512 devices in a mesh: grp: 16 (over y_hi, x, core), seq: 32 (over z, y_lo).
Axes of the slice: x: 4, y: 8 (y_hi: 2, y_lo: 4; y = y_hi * 4 + y_lo), z: 8, core: 2. Of those that a mesh axis runs over, the one named last changes fastest.
Arguments:
- query_vectors: bfloat16 [65536, 1024], P(('grp', 'seq')), may hold values from -140 to 140
- key_vectors: bfloat16 [65536, 1024], P(('grp', 'seq')), may hold values from -5 to 5
- value_vectors: bfloat16 [65536, 1024], P(('grp', 'seq')), may hold values from -6 to 6
- out_grads: bfloat16 [65536, 1024], P(('grp', 'seq')), may hold values from -6 to 6
- offsets: int32 [3, 4], replicated, may hold values from 0 to 127, as said below
Outputs:
- attended: bfloat16 [65536, 1024], P(('grp', 'seq'))
- query_grads: bfloat16 [65536, 1024], P(('grp', 'seq'))
- key_grads: bfloat16 [65536, 1024], P(('grp', 'seq'))
- value_grads: bfloat16 [65536, 1024], P(('grp', 'seq'))
The draws below stay inside these ranges and needn't reach their ends.
Inputs may be any that keep to these rules, and one draw needn't show every extreme that they name: offsets[l, g] lies below the span of far level l + 1, that is 4, 32, 128 for l = 0, 1, 2; some head group has offset 0 at the first far level, and some head group has offset 128 - 1 at the third.
All inputs are finite; a program needn't handle non-finite values.
Results may differ from the reference program's by a relative error of at most 0.011.
Values may be sent and summed in bfloat16 or wider, within the bound.
A program may use at most 64 MiB of HBM per device.

```python
import math
import jax
import jax.numpy as jnp
from jax import lax

HEAD_DIM = 128
HGROUPS = 4
SPAN_A = 4
TOK_DEV = 128
WIDTH = 1024
SPAN_B = 32
SPAN_C = 128
TOKENS = 65536


def shared_keys(key):
    return jnp.clip(jax.random.normal(key, (TOKENS, WIDTH), jnp.float32), -5.0, 5.0)


def draw_key_vectors(key, part):
    source = shared_keys(key)
    return source.astype(jnp.bfloat16)


def draw_query_vectors(key, part):
    key = jax.random.fold_in(key, 3)
    fresh = jnp.clip(jax.random.normal(key, (TOKENS, WIDTH), jnp.float32), -5.0, 5.0)
    return fresh.astype(jnp.bfloat16)


def draw_offsets(key, part):
    key = jax.random.fold_in(key, 7)
    span_list = (SPAN_A, SPAN_B, SPAN_C)
    table = [jax.random.randint(jax.random.fold_in(key, level_id), (HGROUPS,), 0, span_list[level_id], dtype=jnp.int32) for level_id in range(3)]
    group_ids = jnp.arange(HGROUPS, dtype=jnp.int32)
    lowest_group = jax.random.randint(jax.random.fold_in(key, 11), (), 0, HGROUPS, dtype=jnp.int32)
    highest_group = jax.random.randint(jax.random.fold_in(key, 13), (), 0, HGROUPS, dtype=jnp.int32)
    table[0] = jnp.where(group_ids == lowest_group, jnp.int32(0), table[0])
    table[2] = jnp.where(group_ids == highest_group, jnp.int32(SPAN_C - 1), table[2])
    return jnp.stack(table)


def level_of(rng, extent, pieces, smallest, top_value):
    factor_of = 1.0
    for position, shards_of in pieces:
        steps = jax.random.uniform(jax.random.fold_in(jax.random.fold_in(rng, 6), position), (shards_of,), jnp.float32, smallest / len(pieces), top_value / len(pieces))
        factor_of = factor_of * jnp.repeat(jnp.exp(steps), extent[position] // shards_of).reshape((-1,) + (1,) * (len(extent) - 1 - position))
    return factor_of


def gaussian(stream_key, dims, deviation, limit, pieces=(), held_as=jnp.bfloat16):
    array = deviation * jax.random.normal(stream_key, dims, jnp.float32)
    if pieces:
        array = array * level_of(stream_key, dims, pieces, -0.22, 0.18)
    return jnp.clip(array, -limit, limit).astype(held_as)


def setup_inputs(seed: int = 0) -> dict:
    key_list = jax.random.split(jax.random.key(seed), 6)
    query_vectors = draw_query_vectors(jax.random.fold_in(key_list[5], 71), 0)
    key_vectors = draw_key_vectors(jax.random.fold_in(key_list[5], 71), 0)
    value_vectors = gaussian(key_list[2], (TOKENS, WIDTH), 1.0, 6.0, ((0, 512),))
    out_grads = gaussian(key_list[3], (TOKENS, WIDTH), 1.0, 6.0, ((0, 512),))
    offsets = draw_offsets(jax.random.fold_in(key_list[5], 71), 0)
    return dict(query_vectors=query_vectors, key_vectors=key_vectors, value_vectors=value_vectors, out_grads=out_grads, offsets=offsets)


def product(form, left, right):
    return jnp.einsum(form, left.astype(jnp.float32), right.astype(jnp.float32))

def select_tiles(source, offset_row, span_size):
    row_total, feature_count = source.shape
    grouped = source.reshape(row_total // span_size, span_size, HGROUPS, feature_count // HGROUPS)
    selector = (jnp.arange(span_size, dtype=jnp.int32)[:, None] == offset_row[None, :]).astype(source.dtype)
    picked = lax.optimization_barrier(jnp.sum(grouped * selector[None, :, :, None], axis=1))
    return picked.reshape(row_total // span_size, feature_count)

def spread_rows(tile_sums, offset_row, span_size):
    tile_rows, feature_count = tile_sums.shape
    selector = (jnp.arange(span_size, dtype=jnp.int32)[:, None] == offset_row[None, :]).astype(tile_sums.dtype)
    grouped = tile_sums.reshape(tile_rows, 1, HGROUPS, feature_count // HGROUPS) * selector[None, :, :, None]
    return grouped.reshape(tile_rows * span_size, feature_count)

def attend(queries, grads, key_rows, value_rows):
    row_count, feature_count = queries.shape
    level_count = key_rows.shape[0] // row_count
    group_width = feature_count // HGROUPS
    head_count = group_width // HEAD_DIM
    score_scale = 1.0 / math.sqrt(HEAD_DIM)
    results = ([], [], [], [])
    for group_id in range(HGROUPS):
        start_col = group_id * group_width
        query_heads = queries[:, start_col:start_col + group_width].reshape(row_count, head_count, HEAD_DIM)
        grad_heads = grads[:, start_col:start_col + group_width].reshape(row_count, head_count, HEAD_DIM)
        key_heads = key_rows[:, start_col:start_col + group_width].reshape(level_count * row_count, head_count, HEAD_DIM)
        value_heads = value_rows[:, start_col:start_col + group_width].reshape(level_count * row_count, head_count, HEAD_DIM)
        scores = product('ihd,jhd->hij', query_heads, key_heads) * score_scale
        topmost = lax.optimization_barrier(jnp.max(scores, axis=2, keepdims=True))
        powers = jnp.exp(scores - topmost)
        shares = powers / lax.optimization_barrier(jnp.sum(powers, axis=2, keepdims=True))
        weights = shares.astype(jnp.bfloat16)
        blended = product('hij,jhd->ihd', weights, value_heads)
        dshares = product('ihd,jhd->hij', grad_heads, value_heads)
        deltas = lax.optimization_barrier(jnp.sum(grad_heads.astype(jnp.float32) * blended, axis=2))
        dscores = (shares * (dshares - jnp.transpose(deltas)[:, :, None]) * score_scale).astype(jnp.bfloat16)
        results[0].append(blended.reshape(row_count, group_width))
        results[1].append(product('hij,jhd->ihd', dscores, key_heads).reshape(row_count, group_width))
        results[2].append(product('hij,ihd->jhd', dscores, query_heads).reshape(level_count * row_count, group_width))
        results[3].append(product('hij,ihd->jhd', weights, grad_heads).reshape(level_count * row_count, group_width))
    attended = jnp.concatenate(results[0], axis=1).astype(jnp.bfloat16)
    dquery = jnp.concatenate(results[1], axis=1).astype(jnp.bfloat16)
    dkey_rows = jnp.concatenate(results[2], axis=1)
    dvalue_rows = jnp.concatenate(results[3], axis=1)
    return (attended, dquery, dkey_rows, dvalue_rows)

def reference(query_vectors, key_vectors, value_vectors, out_grads, offsets):
    feature_count = query_vectors.shape[1]
    block_count = TOKENS // TOK_DEV
    span_list = (SPAN_A, SPAN_B, SPAN_C)
    key_tiles = [select_tiles(key_vectors, offsets[level_id], span_list[level_id]).reshape(-1, TOK_DEV, feature_count) for level_id in range(3)]
    value_tiles = [select_tiles(value_vectors, offsets[level_id], span_list[level_id]).reshape(-1, TOK_DEV, feature_count) for level_id in range(3)]

    def advance(running, inputs_now):
        block_index, query_block, grad_block, key_block, value_block = inputs_now
        key_sums, value_sums = running
        segment = [block_index // span_size for span_size in span_list]
        key_rows = jnp.concatenate([key_block] + [lax.dynamic_index_in_dim(key_tiles[level_id], segment[level_id], 0, keepdims=False) for level_id in range(3)], axis=0)
        value_rows = jnp.concatenate([value_block] + [lax.dynamic_index_in_dim(value_tiles[level_id], segment[level_id], 0, keepdims=False) for level_id in range(3)], axis=0)
        attended, dquery, dkey_rows, dvalue_rows = attend(query_block, grad_block, key_rows, value_rows)
        key_sums = tuple((key_sums[level_id].at[segment[level_id]].add(dkey_rows[(level_id + 1) * TOK_DEV:(level_id + 2) * TOK_DEV]) for level_id in range(3)))
        value_sums = tuple((value_sums[level_id].at[segment[level_id]].add(dvalue_rows[(level_id + 1) * TOK_DEV:(level_id + 2) * TOK_DEV]) for level_id in range(3)))
        return ((key_sums, value_sums), (attended, dquery, dkey_rows[:TOK_DEV], dvalue_rows[:TOK_DEV]))
    zero_sums = tuple((jnp.zeros((TOKENS // (span_size * TOK_DEV), TOK_DEV, feature_count), jnp.float32) for span_size in span_list))
    inputs_all = (jnp.arange(block_count, dtype=jnp.int32), query_vectors.reshape(block_count, TOK_DEV, feature_count), out_grads.reshape(block_count, TOK_DEV, feature_count), key_vectors.reshape(block_count, TOK_DEV, feature_count), value_vectors.reshape(block_count, TOK_DEV, feature_count))
    (key_sums, value_sums), (attended, dquery, dkey_local, dvalue_local) = lax.scan(advance, (zero_sums, zero_sums), inputs_all)
    key_grads = dkey_local.reshape(TOKENS, feature_count)
    value_grads = dvalue_local.reshape(TOKENS, feature_count)
    for level_id in range(3):
        key_grads = key_grads + spread_rows(key_sums[level_id].reshape(-1, feature_count), offsets[level_id], span_list[level_id])
        value_grads = value_grads + spread_rows(value_sums[level_id].reshape(-1, feature_count), offsets[level_id], span_list[level_id])
    return (attended.reshape(TOKENS, feature_count), dquery.reshape(TOKENS, feature_count), key_grads.astype(jnp.bfloat16), value_grads.astype(jnp.bfloat16))
```

```python
import math

import jax
import jax.numpy as jnp
from jax import lax
from jax.experimental import pallas as pl
from jax.experimental.pallas import tpu as pltpu
from jax.sharding import PartitionSpec as P

MESH = pl.DeviceIdType.MESH
BF = jnp.bfloat16
F32 = jnp.float32
HD = 128
GROUPS = 4
TOK = 128
WIDTH = 1024
NY = 4
NZ = 8
NE = 4
SCALE = 1.0 / math.sqrt(HD)

Y1, Y2, Y3, Z2, Z3, E3 = 0, 3, 6, 9, 16, 23
FAMILY = 26


def mm(a, b):
    return jnp.dot(a, b, preferred_element_type=F32)


def mm_nt(a, b):
    return lax.dot_general(a, b, (((1,), (1,)), ((), ())), preferred_element_type=F32)


def mm_tn(a, b):
    return lax.dot_general(a, b, (((0,), (0,)), ((), ())), preferred_element_type=F32)


def iotas(shape):
    return (
        lax.broadcasted_iota(jnp.int32, shape, 0),
        lax.broadcasted_iota(jnp.int32, shape, 1),
    )


def onehot(mask):
    return jnp.where(mask, 1.0, 0.0).astype(BF)


def kernel(
    off, q_ref, k_ref, v_ref, do_ref,
    o_ref, dq_ref, dk_ref, dv_ref,
    a1, a2, a3, t3, kv2,
    dkv2, b1s, b1r, b2s, b2r, c2s, c2r, b3s, b3r, c3s, c3r, d3s, d3r,
    dk0, dv0, p2, p2t, p3, p3t,
    send_sem, recv_sem,
):
    grp = lax.axis_index("grp")
    seq = lax.axis_index("seq")
    z = seq // NY
    y = seq % NY

    def y_up(k):
        return (grp, z * NY + (y + k) % NY)

    def y_down(k):
        return (grp, z * NY + (y + NY - k) % NY)

    def z_up(m):
        return (grp, (z + m) % NZ * NY + y)

    def z_down(m):
        return (grp, (z + NZ - m) % NZ * NY + y)

    def partner(e):
        low = grp % NE
        bit0 = (low % 2 + e % 2) % 2
        bit1 = (low // 2 + e // 2) % 2
        return (grp // NE * NE + bit1 * 2 + bit0, seq)

    started = []

    def send(src, dst, index, device):
        copy = pltpu.make_async_remote_copy(
            src_ref=src, dst_ref=dst,
            send_sem=send_sem.at[index], recv_sem=recv_sem.at[index],
            device_id=device, device_id_type=MESH,
        )
        copy.start()
        started.append(copy)
        return copy

    barrier = pltpu.get_barrier_semaphore()
    peers = [y_up(k) for k in range(1, NY)]
    peers += [z_up(m) for m in range(1, NZ)]
    peers += [partner(e) for e in range(1, NE)]
    for peer in peers:
        pl.semaphore_signal(barrier, inc=1, device_id=peer, device_id_type=MESH)

    row, col = iotas((16, TOK))
    acc3 = jnp.zeros((16, HD), F32)
    acc2 = jnp.zeros((16, 512), F32)
    for g in range(GROUPS):
        pick = onehot((row // 4 == g) & (col == 32 * (row % 4) + off[1, g]))
        wide = slice(g * 256, g * 256 + 256)
        both = jnp.concatenate([k_ref[:, wide], v_ref[:, wide]], axis=1)
        acc2 += mm(pick, both)
        for hh in range(2):
            h = 2 * g + hh
            cols = slice(h * HD, h * HD + HD)
            acc3 += mm(onehot((row == h) & (col == off[2, g])), k_ref[:, cols])
            acc3 += mm(onehot((row == 8 + h) & (col == off[2, g])), v_ref[:, cols])
    a3[0, 0] = acc3.astype(BF)
    a2[0, 0] = acc2.astype(BF)
    row, col = iotas((32, TOK))
    for g in range(GROUPS):
        pick = onehot(col == 4 * row + off[0, g])
        wide = slice(g * 256, g * 256 + 256)
        a1[0, 0, :, wide] = mm(pick, k_ref[:, wide]).astype(BF)
        a1[0, 1, :, wide] = mm(pick, v_ref[:, wide]).astype(BF)
    row, col = iotas((512, 512))
    p3[...] = onehot(col == row % 32 * 16 + row // 32)
    p3t[...] = onehot(row == col % 32 * 16 + col // 32)
    p2[...] = onehot(col == row % 128 // 4 * 16 + row // 128 * 4 + row % 4)
    p2t[...] = onehot(row == col % 128 // 4 * 16 + col // 128 * 4 + col % 4)

    pl.semaphore_wait(barrier, len(peers))

    fwd_y3 = [send(a3.at[0, 0], a3.at[0, k], Y3 + k - 1, y_up(k)) for k in range(1, NY)]
    fwd_y2 = [send(a2.at[0, 0], a2.at[0, k], Y2 + k - 1, y_up(k)) for k in range(1, NY)]
    fwd_y1 = [send(a1.at[0], a1.at[k], Y1 + k - 1, y_up(k)) for k in range(1, NY)]
    for copy in fwd_y3:
        copy.wait_recv()
    fwd_z3 = [send(a3.at[0], a3.at[m], Z3 + m - 1, z_up(m)) for m in range(1, NZ)]
    for copy in fwd_y2:
        copy.wait_recv()
    fwd_z2 = [send(a2.at[0], a2.at[m], Z2 + m - 1, z_up(m)) for m in range(1, NZ)]
    for copy in fwd_z3:
        copy.wait_recv()
    t3[0] = mm(p3[...], a3[...].reshape(512, HD)).astype(BF)
    fwd_e3 = [send(t3.at[0], t3.at[e], E3 + e - 1, partner(e)) for e in range(1, NE)]
    for copy in fwd_y1 + fwd_e3 + fwd_z2:
        copy.wait_recv()
    kv2[...] = mm(p2[...], a2[...].reshape(512, 512)).astype(BF)

    for h in range(8):
        g, hh = h // 2, h % 2
        cols = slice(h * HD, h * HD + HD)
        rows2 = slice(g * TOK, g * TOK + TOK)
        kcol2 = slice(hh * HD, hh * HD + HD)
        vcol2 = slice(256 + hh * HD, 256 + hh * HD + HD)
        krow3 = slice(h * 32, h * 32 + 32)
        vrow3 = slice(256 + h * 32, 256 + h * 32 + 32)
        q = q_ref[:, cols]
        do = do_ref[:, cols]
        keys = jnp.concatenate(
            [
                k_ref[:, cols], a1[:, 0, :, cols].reshape(TOK, HD),
                kv2[rows2, kcol2], t3[:, krow3, :].reshape(TOK, HD),
            ],
            axis=0,
        )
        values = jnp.concatenate(
            [
                v_ref[:, cols], a1[:, 1, :, cols].reshape(TOK, HD),
                kv2[rows2, vcol2], t3[:, vrow3, :].reshape(TOK, HD),
            ],
            axis=0,
        )
        scores = mm_nt(q, keys) * SCALE
        powers = jnp.exp(scores - jnp.max(scores, axis=1, keepdims=True))
        shares = powers * (1.0 / jnp.sum(powers, axis=1, keepdims=True))
        weights = shares.astype(BF)
        blended = mm(weights, values)
        dshares = mm_nt(do, values)
        deltas = jnp.sum(do.astype(F32) * blended, axis=1, keepdims=True)
        dscores = (shares * (dshares - deltas) * SCALE).astype(BF)
        o_ref[:, cols] = blended.astype(BF)
        dq_ref[:, cols] = mm(dscores, keys).astype(BF)
        dkeys = mm_tn(dscores, q)
        dvalues = mm_tn(weights, do)
        dk0[:, cols] = dkeys[:TOK]
        dv0[:, cols] = dvalues[:TOK]
        b1s[:, 0, :, cols] = dkeys[TOK : 2 * TOK].reshape(NY, 32, HD).astype(BF)
        b1s[:, 1, :, cols] = dvalues[TOK : 2 * TOK].reshape(NY, 32, HD).astype(BF)
        dkv2[rows2, kcol2] = dkeys[2 * TOK : 3 * TOK].astype(BF)
        dkv2[rows2, vcol2] = dvalues[2 * TOK : 3 * TOK].astype(BF)
        b3s[:, krow3, :] = dkeys[3 * TOK :].reshape(NE, 32, HD).astype(BF)
        b3s[:, vrow3, :] = dvalues[3 * TOK :].reshape(NE, 32, HD).astype(BF)

    back = FAMILY
    bwd_e3 = [send(b3s.at[e], b3r.at[e], back + E3 + e - 1, partner(e)) for e in range(1, NE)]
    b2s[...] = mm(p2t[...], dkv2[...]).astype(BF).reshape(NZ, NY, 16, 512)
    bwd_z2 = [send(b2s.at[m], b2r.at[m], back + Z2 + m - 1, z_down(m)) for m in range(1, NZ)]
    bwd_y1 = [send(b1s.at[k], b1r.at[k], back + Y1 + k - 1, y_down(k)) for k in range(1, NY)]
    for copy in bwd_e3:
        copy.wait_recv()
    total3 = b3s[0].astype(F32)
    for e in range(1, NE):
        total3 += b3r[e].astype(F32)
    c3s[...] = mm(p3t[...], total3.astype(BF)).astype(BF).reshape(NZ, NY, 16, HD)
    bwd_z3 = [send(c3s.at[m], c3r.at[m], back + Z3 + m - 1, z_down(m)) for m in range(1, NZ)]
    for copy in bwd_z2:
        copy.wait_recv()
    total2 = b2s[0].astype(F32)
    for m in range(1, NZ):
        total2 += b2r[m].astype(F32)
    c2s[...] = total2.astype(BF)
    bwd_y2 = [send(c2s.at[k], c2r.at[k], back + Y2 + k - 1, y_down(k)) for k in range(1, NY)]
    for copy in bwd_z3:
        copy.wait_recv()
    total3 = c3s[0].astype(F32)
    for m in range(1, NZ):
        total3 += c3r[m].astype(F32)
    d3s[...] = total3.astype(BF)
    bwd_y3 = [send(d3s.at[k], d3r.at[k], back + Y3 + k - 1, y_down(k)) for k in range(1, NY)]

    for copy in bwd_y1:
        copy.wait_recv()
    b1r[0] = b1s[0]
    for copy in bwd_y2:
        copy.wait_recv()
    c2r[0] = c2s[0]
    for copy in bwd_y3:
        copy.wait_recv()
    sums3 = d3s[0].astype(F32)
    for k in range(1, NY):
        sums3 += d3r[k].astype(F32)
    sums2 = c2r[...].reshape(NY * 16, 512)
    row1, col1 = iotas((TOK, TOK))
    row2, col2 = iotas((TOK, NY * 16))
    row3, _ = iotas((TOK, HD))
    for g in range(GROUPS):
        wide = slice(g * 256, g * 256 + 256)
        place1 = onehot(row1 == 4 * (col1 % 32) + off[0, g])
        place2 = onehot((col2 % 16 // 4 == g) & (row2 == 32 * (col2 % 4) + off[1, g]))
        spread2 = mm(place2, sums2)
        here = row3 == off[2, g]
        for kv, (near, out) in enumerate(((dk0, dk_ref), (dv0, dv_ref))):
            spread3 = jnp.concatenate(
                [
                    jnp.where(here, sums3[kv * 8 + 2 * g + hh][None, :], 0.0)
                    for hh in range(2)
                ],
                axis=1,
            )
            out[:, wide] = (
                near[:, wide]
                + mm(place1, b1r[:, kv, :, wide].reshape(TOK, 256))
                + spread2[:, kv * 256 : kv * 256 + 256]
                + spread3
            ).astype(BF)

    for copy in started:
        copy.wait_send()


def on_device(query_vectors, key_vectors, value_vectors, out_grads, offsets):
    vmem = pl.BlockSpec(memory_space=pltpu.VMEM)
    shape = jax.ShapeDtypeStruct((TOK, WIDTH), BF)
    half = lambda *dims: pltpu.VMEM(dims, BF)
    return pl.pallas_call(
        kernel,
        out_shape=(shape,) * 4,
        in_specs=[pl.BlockSpec(memory_space=pltpu.SMEM)] + [vmem] * 4,
        out_specs=(vmem,) * 4,
        scratch_shapes=[
            half(NY, 2, 32, WIDTH),
            half(NZ, NY, 16, 512),
            half(NZ, NY, 16, HD),
            half(NE, 512, HD),
            half(512, 512),
            half(512, 512),
            half(NY, 2, 32, WIDTH),
            half(NY, 2, 32, WIDTH),
            half(NZ, NY, 16, 512),
            half(NZ, NY, 16, 512),
            half(NY, 16, 512),
            half(NY, 16, 512),
            half(NE, 512, HD),
            half(NE, 512, HD),
            half(NZ, NY, 16, HD),
            half(NZ, NY, 16, HD),
            half(NY, 16, HD),
            half(NY, 16, HD),
            pltpu.VMEM((TOK, WIDTH), F32),
            pltpu.VMEM((TOK, WIDTH), F32),
            half(512, 512),
            half(512, 512),
            half(512, 512),
            half(512, 512),
            pltpu.SemaphoreType.DMA((2 * FAMILY,)),
            pltpu.SemaphoreType.DMA((2 * FAMILY,)),
        ],
        compiler_params=pltpu.CompilerParams(
            collective_id=0, has_side_effects=True, vmem_limit_bytes=40 * 1024 * 1024
        ),
        cost_estimate=pl.CostEstimate(
            flops=1_500_000_000, bytes_accessed=2 * 1024 * 1024, transcendentals=524288
        ),
    )(offsets, query_vectors, key_vectors, value_vectors, out_grads)


def solution(mesh):
    rows = P(("grp", "seq"), None)
    return jax.shard_map(
        on_device,
        mesh=mesh,
        in_specs=(rows, rows, rows, rows, P()),
        out_specs=(rows,) * 4,
        check_vma=False,
    )
```

```python
import math

import jax
import jax.numpy as jnp
from jax import lax
from jax.experimental import pallas as pl
from jax.experimental.pallas import tpu as pltpu
from jax.sharding import PartitionSpec as P

MESH = pl.DeviceIdType.MESH
BF = jnp.bfloat16
F32 = jnp.float32
HD = 128
GROUPS = 4
TOK = 128
WIDTH = 1024
NY = 4
NZ = 8
NE = 4
SCALE = 1.0 / math.sqrt(HD)

Y3, Y2, Y1, Z3, Z2, E3 = 0, 3, 6, 18, 25, 57
FAMILY = 69


def mm(a, b):
    return jnp.dot(a, b, preferred_element_type=F32)


def mm_nt(a, b):
    return lax.dot_general(a, b, (((1,), (1,)), ((), ())), preferred_element_type=F32)


def mm_tn(a, b):
    return lax.dot_general(a, b, (((0,), (0,)), ((), ())), preferred_element_type=F32)


def iotas(shape):
    return (
        lax.broadcasted_iota(jnp.int32, shape, 0),
        lax.broadcasted_iota(jnp.int32, shape, 1),
    )


def onehot(mask):
    return jnp.where(mask, 1.0, 0.0).astype(BF)


def exchange(
    off_hbm, q_hbm, k_hbm, v_hbm, do_hbm,
    o_ref, dq_ref, dk_ref, dv_ref,
    off, q_ref, k_ref, v_ref, do_ref,
    a1, a2, a3, t3,
    b1s, b1r, b2s, b2r, b2t, c2s, c2r, b3s, b3r, c3s, c3r, d3s, d3r,
    dk0, dv0, p2, p2t, p3, p3t, place1, place2,
    load_sem, send_sem, recv_sem,
):
    grp = lax.axis_index("grp")
    seq = lax.axis_index("seq")
    z = seq // NY
    y = seq % NY

    def at_y(k):
        return (grp, z * NY + (y + k + NY) % NY)

    def at_z(m):
        return (grp, (z + m + NZ) % NZ * NY + y)

    def partner(e):
        low = grp % NE
        bit0 = (low % 2 + e % 2) % 2
        bit1 = (low // 2 + e // 2) % 2
        return (grp // NE * NE + bit1 * 2 + bit0, seq)

    barrier = pltpu.get_barrier_semaphore()
    peers = [at_y(k) for k in range(1, NY)]
    peers += [at_z(m) for m in range(1, NZ)]
    peers += [partner(e) for e in range(1, NE)]
    for peer in peers:
        pl.semaphore_signal(barrier, inc=1, device_id=peer, device_id_type=MESH)

    loads = [
        pltpu.make_async_copy(src, dst, load_sem.at[i])
        for i, (src, dst) in enumerate(
            ((off_hbm, off), (k_hbm, k_ref), (v_hbm, v_ref), (q_hbm, q_ref), (do_hbm, do_ref))
        )
    ]
    for load in loads:
        load.start()

    started = []

    def send(src, dst, index, device):
        copy = pltpu.make_async_remote_copy(
            src_ref=src, dst_ref=dst,
            send_sem=send_sem.at[index], recv_sem=recv_sem.at[index],
            device_id=device, device_id_type=MESH,
        )
        copy.start()
        started.append(copy)
        return copy

    row, col = iotas((512, 512))
    p3[...] = onehot(col == row % 32 * 16 + row % 128 // 64 * 8 + row // 128 * 2 + row % 64 // 32)
    p2[...] = onehot(col == row % 128 // 4 * 16 + row // 128 * 4 + row % 4)

    for load in loads[:3]:
        load.wait()
    row, col = iotas((32, TOK))
    acc3 = jnp.zeros((16, HD), F32)
    for g in range(GROUPS):
        acc2 = jnp.zeros((16, HD), F32)
        for c in range(4):
            kv, hh = c // 2, c % 2
            h = 2 * g + hh
            source = (k_ref, v_ref)[kv]
            pick = onehot(
                ((row // 4 == c) & (col == 32 * (row % 4) + off[1, g]))
                | ((row == 16 + kv * 8 + h) & (col == off[2, g]))
            )
            rows = mm(pick, source[:, h * HD : h * HD + HD])
            acc2 += rows[:16]
            acc3 += rows[16:]
        a2[0, g, 0] = acc2.astype(BF)
    a3[0, 0] = acc3.astype(BF)

    pl.semaphore_wait(barrier, len(peers))

    fwd_y3 = [send(a3.at[0, 0], a3.at[0, k], Y3 + k - 1, at_y(k)) for k in range(1, NY)]
    fwd_y2 = [send(a2.at[0, :, 0], a2.at[0, :, k], Y2 + k - 1, at_y(k)) for k in range(1, NY)]
    row, col = iotas((32, TOK))
    fwd_y1 = []
    for g in range(GROUPS):
        pick = onehot(col == 4 * row + off[0, g])
        wide = slice(g * 256, g * 256 + 256)
        a1[0, g, 0] = mm(pick, k_ref[:, wide]).astype(BF)
        a1[0, g, 1] = mm(pick, v_ref[:, wide]).astype(BF)
        fwd_y1.append(
            [send(a1.at[0, g], a1.at[k, g], Y1 + g * 3 + k - 1, at_y(k)) for k in range(1, NY)]
        )

    for copy in fwd_y3:
        copy.wait_recv()
    fwd_z3 = [send(a3.at[0], a3.at[m], Z3 + m - 1, at_z(m)) for m in range(1, NZ)]
    for copy in fwd_y2:
        copy.wait_recv()
    fwd_z2 = []
    for g in range(GROUPS):
        base = Z2 + g * 8
        fwd_z2.append(
            [
                send(a2.at[0, g], a2.at[2, g], base, at_z(2)),
                send(a2.at[0, g], a2.at[6, g], base + 1, at_z(-2)),
                send(a2.at[0, g], a2.at[1, g], base + 2, at_z(1)),
                send(a2.at[0, g], a2.at[7, g], base + 3, at_z(-1)),
            ]
        )

    row, col = iotas((512, 512))
    p3t[...] = onehot(row == col % 32 * 16 + col % 128 // 64 * 8 + col // 128 * 2 + col % 64 // 32)
    p2t[...] = onehot(row == col % 128 // 4 * 16 + col // 128 * 4 + col % 4)
    row1, col1 = iotas((TOK, TOK))
    row2, col2 = iotas((512, NY * 16))
    for g in range(GROUPS):
        place1[g] = onehot(row1 == 4 * (col1 % 32) + off[0, g])
        place2[g] = onehot(
            (col2 % 16 // 4 == row2 // 128) & (row2 % 128 == 32 * (col2 % 4) + off[1, g])
        )
    for load in loads[3:]:
        load.wait()

    for copy in fwd_z3:
        copy.wait_recv()
    t3[0] = mm(p3[...], a3[...].reshape(512, HD)).astype(BF).reshape(GROUPS, TOK, HD)
    fwd_e3 = []
    for g in range(GROUPS):
        fwd_e3.append(
            [send(t3.at[0, g], t3.at[e, g], E3 + g * 3 + e - 1, partner(e)) for e in range(1, NE)]
        )
    half = pl.ds(0, 2)
    rest = pl.ds(2, 2)
    for g in range(GROUPS):
        base = Z2 + g * 8
        fwd_z2[g][0].wait_recv()
        fwd_z2[g][1].wait_recv()
        fwd_z2[g] = fwd_z2[g][2:] + [
            send(a2.at[2, g], a2.at[3, g], base + 4, at_z(1)),
            send(a2.at[6, g], a2.at[5, g], base + 5, at_z(-1)),
            send(a2.at[2, g, half], a2.at[4, g, half], base + 6, at_z(2)),
            send(a2.at[6, g, rest], a2.at[4, g, rest], base + 7, at_z(-2)),
        ]

    back = FAMILY
    bwd_e3, bwd_z2, bwd_y1 = [], [], []
    for g in range(GROUPS):
        for copy in fwd_y1[g] + fwd_z2[g] + fwd_e3[g]:
            copy.wait_recv()
        tile2 = mm(p2[...], a2[:, g].reshape(512, HD)).astype(BF)
        grads2 = [None] * 4
        for hh in range(2):
            h = 2 * g + hh
            cols = slice(h * HD, h * HD + HD)
            part = slice(hh * HD, hh * HD + HD)
            krow3 = slice(hh * 32, hh * 32 + 32)
            vrow3 = slice(64 + hh * 32, 64 + hh * 32 + 32)
            q = q_ref[:, cols]
            do = do_ref[:, cols]
            keys = jnp.concatenate(
                [
                    k_ref[:, cols],
                    a1[:, g, 0, :, part].reshape(TOK, HD),
                    tile2[hh * TOK : hh * TOK + TOK],
                    t3[:, g, krow3, :].reshape(TOK, HD),
                ],
                axis=0,
            )
            values = jnp.concatenate(
                [
                    v_ref[:, cols],
                    a1[:, g, 1, :, part].reshape(TOK, HD),
                    tile2[256 + hh * TOK : 256 + hh * TOK + TOK],
                    t3[:, g, vrow3, :].reshape(TOK, HD),
                ],
                axis=0,
            )
            scores = mm_nt(q, keys) * SCALE
            powers = jnp.exp(scores - jnp.max(scores, axis=1, keepdims=True))
            shares = powers * (1.0 / jnp.sum(powers, axis=1, keepdims=True))
            weights = shares.astype(BF)
            blended = mm(weights, values)
            dshares = mm_nt(do, values)
            deltas = jnp.sum(do.astype(F32) * blended, axis=1, keepdims=True)
            dscores = (shares * (dshares - deltas) * SCALE).astype(BF)
            dkeys = mm_tn(dscores, q)
            dvalues = mm_tn(weights, do)
            b3s[:, g, krow3, :] = dkeys[3 * TOK :].reshape(NE, 32, HD).astype(BF)
            b3s[:, g, vrow3, :] = dvalues[3 * TOK :].reshape(NE, 32, HD).astype(BF)
            b1s[:, g, 0, :, part] = dkeys[TOK : 2 * TOK].reshape(NY, 32, HD).astype(BF)
            b1s[:, g, 1, :, part] = dvalues[TOK : 2 * TOK].reshape(NY, 32, HD).astype(BF)
            grads2[hh] = dkeys[2 * TOK : 3 * TOK].astype(BF)
            grads2[2 + hh] = dvalues[2 * TOK : 3 * TOK].astype(BF)
            dk0[:, cols] = dkeys[:TOK]
            dv0[:, cols] = dvalues[:TOK]
            o_ref[:, cols] = blended.astype(BF)
            dq_ref[:, cols] = mm(dscores, keys).astype(BF)
        bwd_e3.append(
            [
                send(b3s.at[e, g], b3r.at[e, g], back + E3 + g * 3 + e - 1, partner(e))
                for e in range(1, NE)
            ]
        )
        bwd_y1.append(
            [
                send(b1s.at[k, g], b1r.at[k, g], back + Y1 + g * 3 + k - 1, at_y(-k))
                for k in range(1, NY)
            ]
        )
        b2s[:, g] = (
            mm(p2t[...], jnp.concatenate(grads2, axis=0)).astype(BF).reshape(NZ, NY, 16, HD)
        )
        base = back + Z2 + g * 8
        bwd_z2.append(
            [
                send(b2s.at[4, g, half], b2r.at[4, g, half], base, at_z(-2)),
                send(b2s.at[4, g, rest], b2r.at[4, g, rest], base + 1, at_z(2)),
                send(b2s.at[3, g], b2r.at[3, g], base + 2, at_z(-1)),
                send(b2s.at[5, g], b2r.at[5, g], base + 3, at_z(1)),
                send(b2s.at[1, g], b2r.at[1, g], base + 4, at_z(-1)),
                send(b2s.at[7, g], b2r.at[7, g], base + 5, at_z(1)),
            ]
        )

    def relay(g):
        for copy in bwd_z2[g][:4]:
            copy.wait_recv()
        base = back + Z2 + g * 8
        low = b2s[2, g].astype(F32) + b2r[3, g].astype(F32)
        high = b2s[6, g].astype(F32) + b2r[5, g].astype(F32)
        b2t[0, g, half] = (low[:2] + b2r[4, g, half].astype(F32)).astype(BF)
        b2t[0, g, rest] = low[2:].astype(BF)
        b2t[1, g, half] = high[:2].astype(BF)
        b2t[1, g, rest] = (high[2:] + b2r[4, g, rest].astype(F32)).astype(BF)
        bwd_z2[g] = bwd_z2[g][4:] + [
            send(b2t.at[0, g], b2r.at[2, g], base + 6, at_z(-2)),
            send(b2t.at[1, g], b2r.at[6, g], base + 7, at_z(2)),
        ]

    relay(0)
    relay(1)
    for copies in bwd_e3:
        for copy in copies:
            copy.wait_recv()
    total3 = b3s[0].astype(F32)
    for e in range(1, NE):
        total3 += b3r[e].astype(F32)
    c3s[...] = (
        mm(p3t[...], total3.astype(BF).reshape(512, HD)).astype(BF).reshape(NZ, NY, 16, HD)
    )
    bwd_z3 = [send(c3s.at[m], c3r.at[m], back + Z3 + m - 1, at_z(-m)) for m in range(1, NZ)]
    relay(2)
    relay(3)
    count = len(started)
    for g in range(GROUPS):
        for copy in bwd_y1[g]:
            copy.wait_recv()
        wide = slice(g * 256, g * 256 + 256)
        for kv, near in enumerate((dk0, dv0)):
            sums1 = jnp.concatenate([b1s[0, g, kv], b1r[1:, g, kv].reshape(96, 256)], axis=0)
            near[:, wide] += mm(place1[g], sums1)
    for g in range(GROUPS):
        for copy in bwd_z2[g]:
            copy.wait_recv()
        total2 = b2s[0, g].astype(F32)
        for m in (1, 2, 6, 7):
            total2 += b2r[m, g].astype(F32)
        c2s[:, g] = total2.astype(BF)
    bwd_y2 = [send(c2s.at[k], c2r.at[k], back + Y2 + k - 1, at_y(-k)) for k in range(1, NY)]
    for copy in bwd_z3:
        copy.wait_recv()
    total3 = c3s[0].astype(F32)
    for m in range(1, NZ):
        total3 += c3r[m].astype(F32)
    d3s[...] = total3.astype(BF)
    bwd_y3 = [send(d3s.at[k], d3r.at[k], back + Y3 + k - 1, at_y(-k)) for k in range(1, NY)]

    for copy in started[:count]:
        copy.wait_send()
    for copy in bwd_y2:
        copy.wait_recv()
    for g in range(GROUPS):
        sums2 = jnp.concatenate([c2s[0, g], c2r[1:, g].reshape(48, HD)], axis=0)
        spread2 = mm(place2[g], sums2)
        for hh in range(2):
            cols = slice((2 * g + hh) * HD, (2 * g + hh) * HD + HD)
            dk0[:, cols] += spread2[hh * TOK : hh * TOK + TOK]
            dv0[:, cols] += spread2[256 + hh * TOK : 256 + hh * TOK + TOK]
    for copy in bwd_y3:
        copy.wait_recv()
    sums3 = d3s[0].astype(F32)
    for k in range(1, NY):
        sums3 += d3r[k].astype(F32)
    row3, _ = iotas((TOK, HD))
    for h in range(8):
        cols = slice(h * HD, h * HD + HD)
        here = row3 == off[2, h // 2]
        dk_ref[:, cols] = (dk0[:, cols] + jnp.where(here, sums3[h][None, :], 0.0)).astype(BF)
        dv_ref[:, cols] = (dv0[:, cols] + jnp.where(here, sums3[8 + h][None, :], 0.0)).astype(BF)

    for copy in started[count:]:
        copy.wait_send()


def write_out(*refs):
    sources, targets, held, load_sem, store_sem = refs[:4], refs[4:8], refs[8], refs[9], refs[10]
    loads = [
        pltpu.make_async_copy(src, held.at[i], load_sem.at[i]) for i, src in enumerate(sources)
    ]
    stores = [
        pltpu.make_async_copy(held.at[i], dst, store_sem.at[i]) for i, dst in enumerate(targets)
    ]
    for load in loads:
        load.start()
    for load, store in zip(loads, stores):
        load.wait()
        store.start()
    for store in stores:
        store.wait()


def on_device(query_vectors, key_vectors, value_vectors, out_grads, offsets):
    vmem = pl.BlockSpec(memory_space=pltpu.VMEM)
    anywhere = pl.BlockSpec(memory_space=pl.ANY)
    shape = jax.ShapeDtypeStruct((TOK, WIDTH), BF)
    half = lambda *dims: pltpu.VMEM(dims, BF)
    results = pl.pallas_call(
        exchange,
        out_shape=(shape,) * 4,
        in_specs=[anywhere] * 5,
        out_specs=(vmem,) * 4,
        scratch_shapes=[
            pltpu.SMEM((3, GROUPS), jnp.int32),
            half(TOK, WIDTH),
            half(TOK, WIDTH),
            half(TOK, WIDTH),
            half(TOK, WIDTH),
            half(NY, GROUPS, 2, 32, 256),
            half(NZ, GROUPS, NY, 16, HD),
            half(NZ, NY, 16, HD),
            half(NE, GROUPS, TOK, HD),
            half(NY, GROUPS, 2, 32, 256),
            half(NY, GROUPS, 2, 32, 256),
            half(NZ, GROUPS, NY, 16, HD),
            half(NZ, GROUPS, NY, 16, HD),
            half(2, GROUPS, NY, 16, HD),
            half(NY, GROUPS, 16, HD),
            half(NY, GROUPS, 16, HD),
            half(NE, GROUPS, TOK, HD),
            half(NE, GROUPS, TOK, HD),
            half(NZ, NY, 16, HD),
            half(NZ, NY, 16, HD),
            half(NY, 16, HD),
            half(NY, 16, HD),
            pltpu.VMEM((TOK, WIDTH), F32),
            pltpu.VMEM((TOK, WIDTH), F32),
            half(512, 512),
            half(512, 512),
            half(512, 512),
            half(512, 512),
            half(GROUPS, TOK, TOK),
            half(GROUPS, 512, NY * 16),
            pltpu.SemaphoreType.DMA((5,)),
            pltpu.SemaphoreType.DMA((2 * FAMILY,)),
            pltpu.SemaphoreType.DMA((2 * FAMILY,)),
        ],
        compiler_params=pltpu.CompilerParams(
            collective_id=0, has_side_effects=True, vmem_limit_bytes=56 * 1024 * 1024
        ),
        cost_estimate=pl.CostEstimate(
            flops=1_500_000_000, bytes_accessed=2 * 1024 * 1024, transcendentals=524288
        ),
    )(offsets, query_vectors, key_vectors, value_vectors, out_grads)
    return pl.pallas_call(
        write_out,
        out_shape=(shape,) * 4,
        in_specs=[anywhere] * 4,
        out_specs=(anywhere,) * 4,
        scratch_shapes=[
            half(4, TOK, WIDTH),
            pltpu.SemaphoreType.DMA((4,)),
            pltpu.SemaphoreType.DMA((4,)),
        ],
        compiler_params=pltpu.CompilerParams(vmem_limit_bytes=60 * 1024 * 1024),
        cost_estimate=pl.CostEstimate(
            flops=0, bytes_accessed=2 * 1024 * 1024, transcendentals=0
        ),
    )(*results)


def solution(mesh):
    rows = P(("grp", "seq"), None)
    return jax.shard_map(
        on_device,
        mesh=mesh,
        in_specs=(rows, rows, rows, rows, P()),
        out_specs=(rows,) * 4,
        check_vma=False,
    )
```

```python
import math

import jax
import jax.numpy as jnp
from jax import lax
from jax.experimental import pallas as pl
from jax.experimental.pallas import tpu as pltpu
from jax.sharding import PartitionSpec as P

MESH = pl.DeviceIdType.MESH
BF = jnp.bfloat16
F32 = jnp.float32
HD = 128
GROUPS = 4
TOK = 128
WIDTH = 1024
NY = 4
NZ = 8
NE = 4
SCALE = 1.0 / math.sqrt(HD)

S3, Y2, Y1, Z2, E3 = 0, 32, 35, 47, 79
FAMILY = 91
DIRECT_F = (0, 1, 2, 3)
DIRECT_B = ()
OTHERS = [(m, k) for m in (4, 3, 5, 2, 6, 1, 7, 0) for k in (3, 2, 1, 0) if (m, k) != (0, 0)]


def mm(a, b):
    return jnp.dot(a, b, preferred_element_type=F32)


def mm_nt(a, b):
    return lax.dot_general(a, b, (((1,), (1,)), ((), ())), preferred_element_type=F32)


def mm_tn(a, b):
    return lax.dot_general(a, b, (((0,), (0,)), ((), ())), preferred_element_type=F32)


def iotas(shape):
    return (
        lax.broadcasted_iota(jnp.int32, shape, 0),
        lax.broadcasted_iota(jnp.int32, shape, 1),
    )


def onehot(mask):
    return jnp.where(mask, 1.0, 0.0).astype(BF)


def exchange(
    off_hbm, q_hbm, k_hbm, v_hbm, do_hbm,
    o_ref, dq_ref, dk_ref, dv_ref,
    off, q_ref, k_ref, v_ref, do_ref,
    a1, a2, a3, t3, kv2, kept_w, kept_d,
    b1s, b1r, b2s, b2r, b2t, c2s, c2r, b3s, b3r, c3s, c3r,
    own_s, own_d, dk0, dv0, p2, p2t, p3, p3t, place1, place2,
    load_sem, send_sem, recv_sem,
):
    grp = lax.axis_index("grp")
    seq = lax.axis_index("seq")
    z = seq // NY
    y = seq % NY

    def at_y(k):
        return (grp, z * NY + (y + k + NY) % NY)

    def at_z(m):
        return (grp, (z + m + NZ) % NZ * NY + y)

    def at_zy(m, k):
        return (grp, (z + m + NZ) % NZ * NY + (y + k + NY) % NY)

    def partner(e):
        low = grp % NE
        bit0 = (low % 2 + e % 2) % 2
        bit1 = (low // 2 + e // 2) % 2
        return (grp // NE * NE + bit1 * 2 + bit0, seq)

    loads = [
        pltpu.make_async_copy(src, dst, load_sem.at[i])
        for i, (src, dst) in enumerate(
            ((off_hbm, off), (k_hbm, k_ref), (v_hbm, v_ref), (q_hbm, q_ref), (do_hbm, do_ref))
        )
    ]
    for load in loads:
        load.start()

    barrier = pltpu.get_barrier_semaphore()
    peers = [at_zy(m, k) for m, k in OTHERS]
    peers += [partner(e) for e in range(1, NE)]
    for peer in peers:
        pl.semaphore_signal(barrier, inc=1, device_id=peer, device_id_type=MESH)

    started = []

    def send(src, dst, index, device):
        copy = pltpu.make_async_remote_copy(
            src_ref=src, dst_ref=dst,
            send_sem=send_sem.at[index], recv_sem=recv_sem.at[index],
            device_id=device, device_id_type=MESH,
        )
        copy.start()
        started.append(copy)
        return copy

    for load in loads[:3]:
        load.wait()
    row, col = iotas((32, TOK))
    acc3 = jnp.zeros((16, HD), F32)
    for g in range(GROUPS):
        acc2 = jnp.zeros((16, HD), F32)
        for c in range(4):
            kv, hh = c // 2, c % 2
            h = 2 * g + hh
            source = (k_ref, v_ref)[kv]
            pick = onehot(
                ((row // 4 == c) & (col == 32 * (row % 4) + off[1, g]))
                | ((row == 16 + kv * 8 + h) & (col == off[2, g]))
            )
            rows = mm(pick, source[:, h * HD : h * HD + HD])
            acc2 += rows[:16]
            acc3 += rows[16:]
        a2[0, g, 0] = acc2.astype(BF)
    a3[0, 0] = acc3.astype(BF)

    pl.semaphore_wait(barrier, len(peers))

    fwd_y2 = [send(a2.at[0, :, 0], a2.at[0, :, k], Y2 + k - 1, at_y(k)) for k in range(1, NY)]
    fwd_s3 = [
        send(a3.at[0, 0], a3.at[m, k], S3 + m * NY + k, at_zy(m, k)) for m, k in OTHERS
    ]
    row, col = iotas((32, TOK))
    fwd_y1 = []
    for g in range(GROUPS):
        pick = onehot(col == 4 * row + off[0, g])
        wide = slice(g * 256, g * 256 + 256)
        a1[0, g, 0] = mm(pick, k_ref[:, wide]).astype(BF)
        a1[0, g, 1] = mm(pick, v_ref[:, wide]).astype(BF)
        fwd_y1.append(
            [send(a1.at[0, g], a1.at[k, g], Y1 + g * 3 + k - 1, at_y(k)) for k in range(1, NY)]
        )

    row, col = iotas((512, 512))
    p3[...] = onehot(col == row % 32 * 16 + row % 128 // 64 * 8 + row // 128 * 2 + row % 64 // 32)
    p2[...] = onehot(col == row % 128 // 4 * 16 + row // 128 * 4 + row % 4)

    for copy in fwd_y2:
        copy.wait_recv()
    fwd_z2 = []
    for g in range(GROUPS):
        base = Z2 + g * 8
        if g in DIRECT_F:
            fwd_z2.append(
                [
                    send(a2.at[0, g], a2.at[m, g], base + m, at_z(m))
                    for m in (4, 3, 5, 2, 6, 1, 7)
                ]
            )
            continue
        fwd_z2.append(
            [
                send(a2.at[0, g], a2.at[2, g], base, at_z(2)),
                send(a2.at[0, g], a2.at[6, g], base + 1, at_z(-2)),
                send(a2.at[0, g], a2.at[1, g], base + 2, at_z(1)),
                send(a2.at[0, g], a2.at[7, g], base + 3, at_z(-1)),
            ]
        )

    row, col = iotas((512, 512))
    p3t[...] = onehot(row == col % 32 * 16 + col % 128 // 64 * 8 + col // 128 * 2 + col % 64 // 32)
    p2t[...] = onehot(row == col % 128 // 4 * 16 + col // 128 * 4 + col % 4)
    row1, col1 = iotas((TOK, TOK))
    row2, col2 = iotas((512, NY * 16))
    for g in range(GROUPS):
        place1[g] = onehot(row1 == 4 * (col1 % 32) + off[0, g])
        place2[g] = onehot(
            (col2 % 16 // 4 == row2 // 128) & (row2 % 128 == 32 * (col2 % 4) + off[1, g])
        )
    for load in loads[3:]:
        load.wait()
    for h in range(8):
        cols = slice(h * HD, h * HD + HD)
        own_s[h] = mm_nt(q_ref[:, cols], k_ref[:, cols])
        own_d[h] = mm_nt(do_ref[:, cols], v_ref[:, cols])

    for copy in fwd_s3:
        copy.wait_recv()
    t3[0] = mm(p3[...], a3[...].reshape(512, HD)).astype(BF).reshape(GROUPS, TOK, HD)
    fwd_e3 = []
    for g in range(GROUPS):
        fwd_e3.append(
            [send(t3.at[0, g], t3.at[e, g], E3 + g * 3 + e - 1, partner(e)) for e in range(1, NE)]
        )
    half = pl.ds(0, 2)
    rest = pl.ds(2, 2)
    for g in range(GROUPS):
        if g in DIRECT_F:
            continue
        base = Z2 + g * 8
        fwd_z2[g][0].wait_recv()
        fwd_z2[g][1].wait_recv()
        fwd_z2[g] = fwd_z2[g][2:] + [
            send(a2.at[2, g], a2.at[3, g], base + 4, at_z(1)),
            send(a2.at[6, g], a2.at[5, g], base + 5, at_z(-1)),
            send(a2.at[2, g, half], a2.at[4, g, half], base + 6, at_z(2)),
            send(a2.at[6, g, rest], a2.at[4, g, rest], base + 7, at_z(-2)),
        ]

    def far_rows(g, hh, kv):
        part = slice(hh * HD, hh * HD + HD)
        row2 = (2 * kv + hh) * TOK
        row3 = kv * 64 + hh * 32
        return jnp.concatenate(
            [
                a1[:, g, kv, :, part].reshape(TOK, HD),
                kv2[g, row2 : row2 + TOK],
                t3[:, g, row3 : row3 + 32, :].reshape(TOK, HD),
            ],
            axis=0,
        )

    def finish(g):
        for hh in range(2):
            h = 2 * g + hh
            cols = slice(h * HD, h * HD + HD)
            weights = kept_w[h]
            dscores = kept_d[h]
            keys = jnp.concatenate([k_ref[:, cols], far_rows(g, hh, 0)], axis=0)
            values = jnp.concatenate([v_ref[:, cols], far_rows(g, hh, 1)], axis=0)
            o_ref[:, cols] = mm(weights, values).astype(BF)
            dq_ref[:, cols] = mm(dscores, keys).astype(BF)
            dk0[:, cols] = mm_tn(dscores[:, :TOK], q_ref[:, cols])
            dv0[:, cols] = mm_tn(weights[:, :TOK], do_ref[:, cols])

    back = FAMILY
    bwd_e3, bwd_z2, bwd_y1 = [], [], []
    for g in range(GROUPS):
        for copy in fwd_y1[g] + fwd_z2[g] + fwd_e3[g]:
            copy.wait_recv()
        kv2[g] = mm(p2[...], a2[:, g].reshape(512, HD)).astype(BF)
        grads2 = [None] * 4
        for hh in range(2):
            h = 2 * g + hh
            cols = slice(h * HD, h * HD + HD)
            part = slice(hh * HD, hh * HD + HD)
            krow3 = slice(hh * 32, hh * 32 + 32)
            vrow3 = slice(64 + hh * 32, 64 + hh * 32 + 32)
            q = q_ref[:, cols]
            do = do_ref[:, cols]
            scores = jnp.concatenate([own_s[h], mm_nt(q, far_rows(g, hh, 0))], axis=1) * SCALE
            dshares = jnp.concatenate([own_d[h], mm_nt(do, far_rows(g, hh, 1))], axis=1)
            powers = jnp.exp(scores - jnp.max(scores, axis=1, keepdims=True))
            shares = powers * (1.0 / jnp.sum(powers, axis=1, keepdims=True))
            weights = shares.astype(BF)
            deltas = jnp.sum(weights.astype(F32) * dshares, axis=1, keepdims=True)
            dscores = (shares * (dshares - deltas) * SCALE).astype(BF)
            kept_w[h] = weights
            kept_d[h] = dscores
            dkeys = mm_tn(dscores[:, TOK:], q)
            dvalues = mm_tn(weights[:, TOK:], do)
            b3s[:, g, krow3, :] = dkeys[2 * TOK :].reshape(NE, 32, HD).astype(BF)
            b3s[:, g, vrow3, :] = dvalues[2 * TOK :].reshape(NE, 32, HD).astype(BF)
            b1s[:, g, 0, :, part] = dkeys[:TOK].reshape(NY, 32, HD).astype(BF)
            b1s[:, g, 1, :, part] = dvalues[:TOK].reshape(NY, 32, HD).astype(BF)
            grads2[hh] = dkeys[TOK : 2 * TOK].astype(BF)
            grads2[2 + hh] = dvalues[TOK : 2 * TOK].astype(BF)
        bwd_e3.append(
            [
                send(b3s.at[e, g], b3r.at[e, g], back + E3 + g * 3 + e - 1, partner(e))
                for e in range(1, NE)
            ]
        )
        bwd_y1.append(
            [
                send(b1s.at[k, g], b1r.at[k, g], back + Y1 + g * 3 + k - 1, at_y(-k))
                for k in range(1, NY)
            ]
        )
        b2s[:, g] = (
            mm(p2t[...], jnp.concatenate(grads2, axis=0)).astype(BF).reshape(NZ, NY, 16, HD)
        )
        base = back + Z2 + g * 8
        if g in DIRECT_B:
            bwd_z2.append(
                [
                    send(b2s.at[m, g], b2r.at[m, g], base + m, at_z(-m))
                    for m in (4, 3, 5, 2, 6, 1, 7)
                ]
            )
            continue
        bwd_z2.append(
            [
                send(b2s.at[4, g, half], b2r.at[4, g, half], base, at_z(-2)),
                send(b2s.at[4, g, rest], b2r.at[4, g, rest], base + 1, at_z(2)),
                send(b2s.at[3, g], b2r.at[3, g], base + 2, at_z(-1)),
                send(b2s.at[5, g], b2r.at[5, g], base + 3, at_z(1)),
                send(b2s.at[1, g], b2r.at[1, g], base + 4, at_z(-1)),
                send(b2s.at[7, g], b2r.at[7, g], base + 5, at_z(1)),
            ]
        )

    def relay(g):
        if g in DIRECT_B:
            return
        for copy in bwd_z2[g][:4]:
            copy.wait_recv()
        base = back + Z2 + g * 8
        low = b2s[2, g].astype(F32) + b2r[3, g].astype(F32)
        high = b2s[6, g].astype(F32) + b2r[5, g].astype(F32)
        b2t[0, g, half] = (low[:2] + b2r[4, g, half].astype(F32)).astype(BF)
        b2t[0, g, rest] = low[2:].astype(BF)
        b2t[1, g, half] = high[:2].astype(BF)
        b2t[1, g, rest] = (high[2:] + b2r[4, g, rest].astype(F32)).astype(BF)
        bwd_z2[g] = bwd_z2[g][4:] + [
            send(b2t.at[0, g], b2r.at[2, g], base + 6, at_z(-2)),
            send(b2t.at[1, g], b2r.at[6, g], base + 7, at_z(2)),
        ]

    relay(0)
    relay(1)
    relay(2)
    finish(0)
    finish(1)
    relay(3)
    for copies in bwd_e3:
        for copy in copies:
            copy.wait_recv()
    total3 = b3s[0].astype(F32)
    for e in range(1, NE):
        total3 += b3r[e].astype(F32)
    c3s[...] = (
        mm(p3t[...], total3.astype(BF).reshape(512, HD)).astype(BF).reshape(NZ, NY, 16, HD)
    )
    bwd_s3 = [
        send(c3s.at[m, k], c3r.at[m, k], back + S3 + m * NY + k, at_zy(-m, -k)) for m, k in OTHERS
    ]
    count = len(started)
    for g in range(GROUPS):
        for copy in bwd_z2[g]:
            copy.wait_recv()
        total2 = b2s[0, g].astype(F32)
        for m in range(1, NZ) if g in DIRECT_B else (1, 2, 6, 7):
            total2 += b2r[m, g].astype(F32)
        c2s[:, g] = total2.astype(BF)
    bwd_y2 = [send(c2s.at[k], c2r.at[k], back + Y2 + k - 1, at_y(-k)) for k in range(1, NY)]

    finish(2)
    finish(3)
    for g in range(GROUPS):
        for copy in bwd_y1[g]:
            copy.wait_recv()
        wide = slice(g * 256, g * 256 + 256)
        for kv, near in enumerate((dk0, dv0)):
            sums1 = jnp.concatenate([b1s[0, g, kv], b1r[1:, g, kv].reshape(96, 256)], axis=0)
            near[:, wide] += mm(place1[g], sums1)
    for copy in started[:count]:
        copy.wait_send()
    for copy in bwd_y2:
        copy.wait_recv()
    for g in range(GROUPS):
        sums2 = jnp.concatenate([c2s[0, g], c2r[1:, g].reshape(48, HD)], axis=0)
        spread2 = mm(place2[g], sums2)
        for hh in range(2):
            cols = slice((2 * g + hh) * HD, (2 * g + hh) * HD + HD)
            dk0[:, cols] += spread2[hh * TOK : hh * TOK + TOK]
            dv0[:, cols] += spread2[256 + hh * TOK : 256 + hh * TOK + TOK]
    for copy in bwd_s3:
        copy.wait_recv()
    sums3 = c3s[0, 0].astype(F32)
    for m, k in OTHERS:
        sums3 += c3r[m, k].astype(F32)
    row3, _ = iotas((TOK, HD))
    for h in range(8):
        cols = slice(h * HD, h * HD + HD)
        here = row3 == off[2, h // 2]
        dk_ref[:, cols] = (dk0[:, cols] + jnp.where(here, sums3[h][None, :], 0.0)).astype(BF)
        dv_ref[:, cols] = (dv0[:, cols] + jnp.where(here, sums3[8 + h][None, :], 0.0)).astype(BF)

    for copy in started[count:]:
        copy.wait_send()


def write_out(*refs):
    sources, targets, sem = refs[:4], refs[4:8], refs[8]
    copies = [
        pltpu.make_async_copy(src, dst, sem.at[i])
        for i, (src, dst) in enumerate(zip(sources, targets))
    ]
    for copy in copies:
        copy.start()
    for copy in copies:
        copy.wait()


def on_device(query_vectors, key_vectors, value_vectors, out_grads, offsets):
    vmem = pl.BlockSpec(memory_space=pltpu.VMEM)
    anywhere = pl.BlockSpec(memory_space=pl.ANY)
    shape = jax.ShapeDtypeStruct((TOK, WIDTH), BF)
    half = lambda *dims: pltpu.VMEM(dims, BF)
    results = pl.pallas_call(
        exchange,
        out_shape=(pltpu.VMEM((TOK, WIDTH), BF),) * 4,
        in_specs=[pl.BlockSpec(memory_space=pltpu.HBM)] * 5,
        out_specs=(vmem,) * 4,
        scratch_shapes=[
            pltpu.SMEM((3, GROUPS), jnp.int32),
            half(TOK, WIDTH),
            half(TOK, WIDTH),
            half(TOK, WIDTH),
            half(TOK, WIDTH),
            half(NY, GROUPS, 2, 32, 256),
            half(NZ, GROUPS, NY, 16, HD),
            half(NZ, NY, 16, HD),
            half(NE, GROUPS, TOK, HD),
            half(GROUPS, 512, HD),
            half(8, TOK, 4 * TOK),
            half(8, TOK, 4 * TOK),
            half(NY, GROUPS, 2, 32, 256),
            half(NY, GROUPS, 2, 32, 256),
            half(NZ, GROUPS, NY, 16, HD),
            half(NZ, GROUPS, NY, 16, HD),
            half(2, GROUPS, NY, 16, HD),
            half(NY, GROUPS, 16, HD),
            half(NY, GROUPS, 16, HD),
            half(NE, GROUPS, TOK, HD),
            half(NE, GROUPS, TOK, HD),
            half(NZ, NY, 16, HD),
            half(NZ, NY, 16, HD),
            pltpu.VMEM((8, TOK, TOK), F32),
            pltpu.VMEM((8, TOK, TOK), F32),
            pltpu.VMEM((TOK, WIDTH), F32),
            pltpu.VMEM((TOK, WIDTH), F32),
            half(512, 512),
            half(512, 512),
            half(512, 512),
            half(512, 512),
            half(GROUPS, TOK, TOK),
            half(GROUPS, 512, NY * 16),
            pltpu.SemaphoreType.DMA((5,)),
            pltpu.SemaphoreType.DMA((2 * FAMILY,)),
            pltpu.SemaphoreType.DMA((2 * FAMILY,)),
        ],
        compiler_params=pltpu.CompilerParams(
            collective_id=0, has_side_effects=True, vmem_limit_bytes=56 * 1024 * 1024
        ),
        cost_estimate=pl.CostEstimate(
            flops=1_500_000_000, bytes_accessed=2 * 1024 * 1024, transcendentals=524288
        ),
    )(offsets, query_vectors, key_vectors, value_vectors, out_grads)
    return pl.pallas_call(
        write_out,
        out_shape=(shape,) * 4,
        in_specs=[vmem] * 4,
        out_specs=(anywhere,) * 4,
        scratch_shapes=[pltpu.SemaphoreType.DMA((4,))],
        compiler_params=pltpu.CompilerParams(vmem_limit_bytes=16 * 1024 * 1024),
        cost_estimate=pl.CostEstimate(
            flops=0, bytes_accessed=2 * 1024 * 1024, transcendentals=0
        ),
    )(*results)


def solution(mesh):
    rows = P(("grp", "seq"), None)
    return jax.shard_map(
        on_device,
        mesh=mesh,
        in_specs=(rows, rows, rows, rows, P()),
        out_specs=(rows,) * 4,
        check_vma=False,
    )
```

```python
import math

import jax
import jax.numpy as jnp
from jax import lax
from jax.experimental import pallas as pl
from jax.experimental.pallas import tpu as pltpu
from jax.sharding import PartitionSpec as P

MESH = pl.DeviceIdType.MESH
BF = jnp.bfloat16
F32 = jnp.float32
HD = 128
GROUPS = 4
TOK = 128
WIDTH = 1024
NY = 4
NZ = 8
NE = 4
SCALE = 1.0 / math.sqrt(HD)

S3, Y2, Y1, Z2, E3 = 0, 32, 35, 47, 79
FAMILY = 91
OTHERS = [(m, k) for m in (4, 3, 5, 2, 6, 1, 7, 0) for k in (3, 2, 1, 0) if (m, k) != (0, 0)]


def mm(a, b):
    return jnp.dot(a, b, preferred_element_type=F32)


def mm_nt(a, b):
    return lax.dot_general(a, b, (((1,), (1,)), ((), ())), preferred_element_type=F32)


def mm_tn(a, b):
    return lax.dot_general(a, b, (((0,), (0,)), ((), ())), preferred_element_type=F32)


def iotas(shape):
    return (
        lax.broadcasted_iota(jnp.int32, shape, 0),
        lax.broadcasted_iota(jnp.int32, shape, 1),
    )


def onehot(mask):
    return jnp.where(mask, 1.0, 0.0).astype(BF)


def exchange(
    off_hbm, q_hbm, k_hbm, v_hbm, do_hbm,
    o_ref, dq_ref, dk_ref, dv_ref,
    off, q_ref, k_ref, v_ref, do_ref,
    a1, a2, a3, t3, kv2, kept_w, kept_d,
    b1s, b1r, b2s, b2r, b2t, c2s, c2r, b3s, b3r, c3s, c3r,
    own_s, own_d, dk0, dv0, p2, p2t, p3, p3t, place1, place2,
    load_sem, send_sem, recv_sem,
):
    grp = lax.axis_index("grp")
    seq = lax.axis_index("seq")
    z = seq // NY
    y = seq % NY

    def at_y(k):
        return (grp, z * NY + (y + k + NY) % NY)

    def at_z(m):
        return (grp, (z + m + NZ) % NZ * NY + y)

    def at_zy(m, k):
        return (grp, (z + m + NZ) % NZ * NY + (y + k + NY) % NY)

    def partner(e):
        low = grp % NE
        bit0 = (low % 2 + e % 2) % 2
        bit1 = (low // 2 + e // 2) % 2
        return (grp // NE * NE + bit1 * 2 + bit0, seq)

    barrier = pltpu.get_barrier_semaphore()
    peers = [at_zy(m, k) for m, k in OTHERS]
    peers += [partner(e) for e in range(1, NE)]
    for peer in peers:
        pl.semaphore_signal(barrier, inc=1, device_id=peer, device_id_type=MESH)

    loads = [
        pltpu.make_async_copy(src, dst, load_sem.at[i])
        for i, (src, dst) in enumerate(
            ((off_hbm, off), (k_hbm, k_ref), (v_hbm, v_ref), (q_hbm, q_ref), (do_hbm, do_ref))
        )
    ]
    for load in loads:
        load.start()

    started = []

    def send(src, dst, index, device):
        copy = pltpu.make_async_remote_copy(
            src_ref=src, dst_ref=dst,
            send_sem=send_sem.at[index], recv_sem=recv_sem.at[index],
            device_id=device, device_id_type=MESH,
        )
        copy.start()
        started.append(copy)
        return copy

    row, col = iotas((512, 512))
    p3[...] = onehot(col == row % 32 * 16 + row % 128 // 64 * 8 + row // 128 * 2 + row % 64 // 32)
    for load in loads[:3]:
        load.wait()
    row, col = iotas((32, TOK))
    acc3 = jnp.zeros((16, HD), F32)
    for g in range(GROUPS):
        acc2 = jnp.zeros((16, HD), F32)
        for c in range(4):
            kv, hh = c // 2, c % 2
            h = 2 * g + hh
            source = (k_ref, v_ref)[kv]
            pick = onehot(
                ((row // 4 == c) & (col == 32 * (row % 4) + off[1, g]))
                | ((row == 16 + kv * 8 + h) & (col == off[2, g]))
            )
            rows = mm(pick, source[:, h * HD : h * HD + HD])
            acc2 += rows[:16]
            acc3 += rows[16:]
        a2[0, g, 0] = acc2.astype(BF)
    a3[0, 0] = acc3.astype(BF)

    pl.semaphore_wait(barrier, len(peers))

    fwd_y2 = [send(a2.at[0, :, 0], a2.at[0, :, k], Y2 + k - 1, at_y(k)) for k in range(1, NY)]
    fwd_s3 = [
        send(a3.at[0, 0], a3.at[m, k], S3 + m * NY + k, at_zy(m, k)) for m, k in OTHERS
    ]
    row, col = iotas((32, TOK))
    fwd_y1 = []
    for g in range(GROUPS):
        pick = onehot(col == 4 * row + off[0, g])
        wide = slice(g * 256, g * 256 + 256)
        a1[0, g, 0] = mm(pick, k_ref[:, wide]).astype(BF)
        a1[0, g, 1] = mm(pick, v_ref[:, wide]).astype(BF)
        fwd_y1.append(
            [send(a1.at[0, g], a1.at[k, g], Y1 + g * 3 + k - 1, at_y(k)) for k in range(1, NY)]
        )

    for copy in fwd_y2:
        copy.wait_recv()
    fwd_z2 = []
    for g in range(GROUPS):
        base = Z2 + g * 8
        fwd_z2.append(
            [send(a2.at[0, g], a2.at[m, g], base + m, at_z(m)) for m in (4, 3, 5, 2, 6, 1, 7)]
        )

    for copy in fwd_s3:
        copy.wait_recv()
    t3[0] = mm(p3[...], a3[...].reshape(512, HD)).astype(BF).reshape(GROUPS, TOK, HD)
    fwd_e3 = []
    for g in range(GROUPS):
        fwd_e3.append(
            [send(t3.at[0, g], t3.at[e, g], E3 + g * 3 + e - 1, partner(e)) for e in (2, 3, 1)]
        )
    def far_rows(g, hh, kv):
        part = slice(hh * HD, hh * HD + HD)
        row2 = (2 * kv + hh) * TOK
        row3 = kv * 64 + hh * 32
        return jnp.concatenate(
            [
                a1[:, g, kv, :, part].reshape(TOK, HD),
                kv2[g, row2 : row2 + TOK],
                t3[:, g, row3 : row3 + 32, :].reshape(TOK, HD),
            ],
            axis=0,
        )

    def finish(g):
        for hh in range(2):
            h = 2 * g + hh
            cols = slice(h * HD, h * HD + HD)
            weights = kept_w[h]
            dscores = kept_d[h]
            keys = jnp.concatenate([k_ref[:, cols], far_rows(g, hh, 0)], axis=0)
            values = jnp.concatenate([v_ref[:, cols], far_rows(g, hh, 1)], axis=0)
            o_ref[:, cols] = mm(weights, values).astype(BF)
            dq_ref[:, cols] = mm(dscores, keys).astype(BF)
            dk0[:, cols] = mm_tn(dscores[:, :TOK], q_ref[:, cols])
            dv0[:, cols] = mm_tn(weights[:, :TOK], do_ref[:, cols])

    row, col = iotas((512, 512))
    p2[...] = onehot(col == row % 128 // 4 * 16 + row // 128 * 4 + row % 4)

    p2t[...] = onehot(row == col % 128 // 4 * 16 + col // 128 * 4 + col % 4)
    for load in loads[3:]:
        load.wait()
    for h in range(8):
        cols = slice(h * HD, h * HD + HD)
        own_s[h] = mm_nt(q_ref[:, cols], k_ref[:, cols])
        own_d[h] = mm_nt(do_ref[:, cols], v_ref[:, cols])

    back = FAMILY
    half = pl.ds(0, 2)
    rest = pl.ds(2, 2)
    bwd_e3, bwd_z2, bwd_y1 = [], [], []
    for g in range(GROUPS):
        for copy in fwd_y1[g] + fwd_z2[g] + fwd_e3[g]:
            copy.wait_recv()
        kv2[g] = mm(p2[...], a2[:, g].reshape(512, HD)).astype(BF)
        grads2 = [None] * 4
        for hh in range(2):
            h = 2 * g + hh
            cols = slice(h * HD, h * HD + HD)
            part = slice(hh * HD, hh * HD + HD)
            krow3 = slice(hh * 32, hh * 32 + 32)
            vrow3 = slice(64 + hh * 32, 64 + hh * 32 + 32)
            q = q_ref[:, cols]
            do = do_ref[:, cols]
            scores = jnp.concatenate([own_s[h], mm_nt(q, far_rows(g, hh, 0))], axis=1) * SCALE
            dshares = jnp.concatenate([own_d[h], mm_nt(do, far_rows(g, hh, 1))], axis=1)
            powers = jnp.exp(scores - jnp.max(scores, axis=1, keepdims=True))
            shares = powers * (1.0 / jnp.sum(powers, axis=1, keepdims=True))
            weights = shares.astype(BF)
            deltas = jnp.sum(weights.astype(F32) * dshares, axis=1, keepdims=True)
            dscores = (shares * (dshares - deltas) * SCALE).astype(BF)
            kept_w[h] = weights
            kept_d[h] = dscores
            dkeys = mm_tn(dscores[:, TOK:], q)
            dvalues = mm_tn(weights[:, TOK:], do)
            b3s[:, g, krow3, :] = dkeys[2 * TOK :].reshape(NE, 32, HD).astype(BF)
            b3s[:, g, vrow3, :] = dvalues[2 * TOK :].reshape(NE, 32, HD).astype(BF)
            b1s[:, g, 0, :, part] = dkeys[:TOK].reshape(NY, 32, HD).astype(BF)
            b1s[:, g, 1, :, part] = dvalues[:TOK].reshape(NY, 32, HD).astype(BF)
            grads2[hh] = dkeys[TOK : 2 * TOK].astype(BF)
            grads2[2 + hh] = dvalues[TOK : 2 * TOK].astype(BF)
        bwd_y1.append(
            [
                send(b1s.at[k, g], b1r.at[k, g], back + Y1 + g * 3 + k - 1, at_y(-k))
                for k in range(1, NY)
            ]
        )
        bwd_e3.append(
            [
                send(b3s.at[e, g], b3r.at[e, g], back + E3 + g * 3 + e - 1, partner(e))
                for e in (2, 3, 1)
            ]
        )
        b2s[:, g] = (
            mm(p2t[...], jnp.concatenate(grads2, axis=0)).astype(BF).reshape(NZ, NY, 16, HD)
        )
        base = back + Z2 + g * 8
        bwd_z2.append(
            [
                send(b2s.at[4, g, half], b2r.at[4, g, half], base, at_z(-2)),
                send(b2s.at[4, g, rest], b2r.at[4, g, rest], base + 1, at_z(2)),
                send(b2s.at[3, g], b2r.at[3, g], base + 2, at_z(-1)),
                send(b2s.at[5, g], b2r.at[5, g], base + 3, at_z(1)),
                send(b2s.at[1, g], b2r.at[1, g], base + 4, at_z(-1)),
                send(b2s.at[7, g], b2r.at[7, g], base + 5, at_z(1)),
            ]
        )

    def relay(g):
        for copy in bwd_z2[g][:4]:
            copy.wait_recv()
        base = back + Z2 + g * 8
        low = b2s[2, g].astype(F32) + b2r[3, g].astype(F32)
        high = b2s[6, g].astype(F32) + b2r[5, g].astype(F32)
        b2t[0, g, half] = (low[:2] + b2r[4, g, half].astype(F32)).astype(BF)
        b2t[0, g, rest] = low[2:].astype(BF)
        b2t[1, g, half] = high[:2].astype(BF)
        b2t[1, g, rest] = (high[2:] + b2r[4, g, rest].astype(F32)).astype(BF)
        bwd_z2[g] = bwd_z2[g][4:] + [
            send(b2t.at[0, g], b2r.at[2, g], base + 6, at_z(-2)),
            send(b2t.at[1, g], b2r.at[6, g], base + 7, at_z(2)),
        ]

    relay(0)
    relay(1)
    row, col = iotas((512, 512))
    p3t[...] = onehot(row == col % 32 * 16 + col % 128 // 64 * 8 + col // 128 * 2 + col % 64 // 32)
    relay(2)
    finish(0)
    finish(1)
    relay(3)
    for copies in bwd_e3:
        for copy in copies:
            copy.wait_recv()
    total3 = b3s[0].astype(F32)
    for e in range(1, NE):
        total3 += b3r[e].astype(F32)
    c3s[...] = (
        mm(p3t[...], total3.astype(BF).reshape(512, HD)).astype(BF).reshape(NZ, NY, 16, HD)
    )
    bwd_s3 = [
        send(c3s.at[m, k], c3r.at[m, k], back + S3 + m * NY + k, at_zy(-m, -k)) for m, k in OTHERS
    ]
    count = len(started)
    for g in range(GROUPS):
        for copy in bwd_z2[g]:
            copy.wait_recv()
        total2 = b2s[0, g].astype(F32)
        for m in (1, 2, 6, 7):
            total2 += b2r[m, g].astype(F32)
        c2s[:, g] = total2.astype(BF)
    bwd_y2 = [send(c2s.at[k], c2r.at[k], back + Y2 + k - 1, at_y(-k)) for k in range(1, NY)]

    finish(2)
    finish(3)
    row1, col1 = iotas((TOK, TOK))
    row2, col2 = iotas((512, NY * 16))
    for g in range(GROUPS):
        place1[g] = onehot(row1 == 4 * (col1 % 32) + off[0, g])
        place2[g] = onehot(
            (col2 % 16 // 4 == row2 // 128) & (row2 % 128 == 32 * (col2 % 4) + off[1, g])
        )
    for g in range(GROUPS):
        for copy in bwd_y1[g]:
            copy.wait_recv()
        wide = slice(g * 256, g * 256 + 256)
        for kv, near in enumerate((dk0, dv0)):
            sums1 = jnp.concatenate([b1s[0, g, kv], b1r[1:, g, kv].reshape(96, 256)], axis=0)
            near[:, wide] += mm(place1[g], sums1)
    for copy in started[:count]:
        copy.wait_send()
    for copy in bwd_y2:
        copy.wait_recv()
    for g in range(GROUPS):
        sums2 = jnp.concatenate([c2s[0, g], c2r[1:, g].reshape(48, HD)], axis=0)
        spread2 = mm(place2[g], sums2)
        for hh in range(2):
            cols = slice((2 * g + hh) * HD, (2 * g + hh) * HD + HD)
            dk0[:, cols] += spread2[hh * TOK : hh * TOK + TOK]
            dv0[:, cols] += spread2[256 + hh * TOK : 256 + hh * TOK + TOK]
    for copy in bwd_s3:
        copy.wait_recv()
    sums3 = c3s[0, 0].astype(F32)
    for m, k in OTHERS:
        sums3 += c3r[m, k].astype(F32)
    row3, _ = iotas((TOK, HD))
    for h in range(8):
        cols = slice(h * HD, h * HD + HD)
        here = row3 == off[2, h // 2]
        dk_ref[:, cols] = (dk0[:, cols] + jnp.where(here, sums3[h][None, :], 0.0)).astype(BF)
        dv_ref[:, cols] = (dv0[:, cols] + jnp.where(here, sums3[8 + h][None, :], 0.0)).astype(BF)

    for copy in started[count:]:
        copy.wait_send()


def write_out(*refs):
    sources, targets, sem = refs[:4], refs[4:8], refs[8]
    copies = [
        pltpu.make_async_copy(src, dst, sem.at[i])
        for i, (src, dst) in enumerate(zip(sources, targets))
    ]
    for copy in copies:
        copy.start()
    for copy in copies:
        copy.wait()


def on_device(query_vectors, key_vectors, value_vectors, out_grads, offsets):
    vmem = pl.BlockSpec(memory_space=pltpu.VMEM)
    anywhere = pl.BlockSpec(memory_space=pl.ANY)
    shape = jax.ShapeDtypeStruct((TOK, WIDTH), BF)
    half = lambda *dims: pltpu.VMEM(dims, BF)
    results = pl.pallas_call(
        exchange,
        out_shape=(pltpu.VMEM((TOK, WIDTH), BF),) * 4,
        in_specs=[pl.BlockSpec(memory_space=pltpu.HBM)] * 5,
        out_specs=(vmem,) * 4,
        scratch_shapes=[
            pltpu.SMEM((3, GROUPS), jnp.int32),
            half(TOK, WIDTH),
            half(TOK, WIDTH),
            half(TOK, WIDTH),
            half(TOK, WIDTH),
            half(NY, GROUPS, 2, 32, 256),
            half(NZ, GROUPS, NY, 16, HD),
            half(NZ, NY, 16, HD),
            half(NE, GROUPS, TOK, HD),
            half(GROUPS, 512, HD),
            half(8, TOK, 4 * TOK),
            half(8, TOK, 4 * TOK),
            half(NY, GROUPS, 2, 32, 256),
            half(NY, GROUPS, 2, 32, 256),
            half(NZ, GROUPS, NY, 16, HD),
            half(NZ, GROUPS, NY, 16, HD),
            half(2, GROUPS, NY, 16, HD),
            half(NY, GROUPS, 16, HD),
            half(NY, GROUPS, 16, HD),
            half(NE, GROUPS, TOK, HD),
            half(NE, GROUPS, TOK, HD),
            half(NZ, NY, 16, HD),
            half(NZ, NY, 16, HD),
            pltpu.VMEM((8, TOK, TOK), F32),
            pltpu.VMEM((8, TOK, TOK), F32),
            pltpu.VMEM((TOK, WIDTH), F32),
            pltpu.VMEM((TOK, WIDTH), F32),
            half(512, 512),
            half(512, 512),
            half(512, 512),
            half(512, 512),
            half(GROUPS, TOK, TOK),
            half(GROUPS, 512, NY * 16),
            pltpu.SemaphoreType.DMA((5,)),
            pltpu.SemaphoreType.DMA((2 * FAMILY,)),
            pltpu.SemaphoreType.DMA((2 * FAMILY,)),
        ],
        compiler_params=pltpu.CompilerParams(
            collective_id=0, has_side_effects=True, vmem_limit_bytes=56 * 1024 * 1024
        ),
        cost_estimate=pl.CostEstimate(
            flops=1_500_000_000, bytes_accessed=2 * 1024 * 1024, transcendentals=524288
        ),
    )(offsets, query_vectors, key_vectors, value_vectors, out_grads)
    return pl.pallas_call(
        write_out,
        out_shape=(shape,) * 4,
        in_specs=[vmem] * 4,
        out_specs=(anywhere,) * 4,
        scratch_shapes=[pltpu.SemaphoreType.DMA((4,))],
        compiler_params=pltpu.CompilerParams(vmem_limit_bytes=16 * 1024 * 1024),
        cost_estimate=pl.CostEstimate(
            flops=0, bytes_accessed=2 * 1024 * 1024, transcendentals=0
        ),
    )(*results)


def solution(mesh):
    rows = P(("grp", "seq"), None)
    return jax.shard_map(
        on_device,
        mesh=mesh,
        in_specs=(rows, rows, rows, rows, P()),
        out_specs=(rows,) * 4,
        check_vma=False,
    )
```
